256 devices in a mesh: dp: 32 (over y_hi, z, core), panel: 4 (over x), bin: 2 (over y_lo).
Axes of the slice: x: 4, y: 4 (y_hi: 2, y_lo: 2; y = y_hi * 2 + y_lo), z: 8, core: 2. Of those that a mesh axis runs over, the one named last changes fastest.
Arguments:
- histograms: bfloat16 [393216, 256], P('dp', 'bin'), may hold values from -6 to 6
- first_assign: int32 [393216], P('dp'), may hold values from 0 to 1023
- second_assign: int32 [393216], P('dp'), may hold values from 0 to 1023
- start_centroids: float32 [1024, 256], P('panel', 'bin'), may hold values from -3 to 3
Outputs:
- centroids: float32 [1024, 256], P('panel', 'bin')
- distortion: float32 [393216], P(('dp', 'bin'))
The draws below stay inside these ranges and needn't reach their ends.
All inputs are finite; a program needn't handle non-finite values.
Results may differ from the reference program's by a relative error of at most 0.0015.
Values may be sent and summed in bfloat16 or wider, within the bound.
A program may use at most 64 MiB of HBM per device.

```python
import jax
import jax.numpy as jnp
from jax import lax

BINS = 256
BUCKETS = 1024
ROW_DEV = 12288
ROWS = 393216
PRIOR = 384


def set_ends(drawn, stream_key, smallest, high):
    shape = drawn.shape
    spot = [jax.random.randint(jax.random.fold_in(stream_key, axis), (), 0, shape[axis]) for axis in range(len(shape))]
    drawn = drawn.at[tuple(spot)].set(smallest)
    longest = shape.index(max(shape))
    spot[longest] = (spot[longest] + 1) % shape[longest]
    return drawn.at[tuple(spot)].set(high)


def level_of(key, shape, shards, smallest, top_value):
    factor_of, own = 1.0, jax.random.fold_in(key, 6)
    for axis_at, parts in shards:
        steps = jnp.exp(jax.random.uniform(jax.random.fold_in(own, axis_at), (parts,), jnp.float32, smallest / len(shards), top_value / len(shards)))
        factor_of = factor_of * jnp.repeat(steps, shape[axis_at] // parts).reshape([-1 if axis == axis_at else 1 for axis in range(len(shape))])
    return factor_of


def normal_values(own_key, extent, deviation, most, split=(), held_as=jnp.bfloat16):
    factor_of = level_of(own_key, extent, split, -0.22, 0.18) if split else 1.0
    result = jax.random.normal(own_key, extent, jnp.float32) * deviation * factor_of
    return jnp.minimum(jnp.maximum(result, -most), most).astype(held_as)


def setup_inputs(seed: int = 0) -> dict:
    key_of = jax.random.split(jax.random.key(seed), 5)
    return {
        "histograms": normal_values(key_of[0], (ROWS, BINS), 1.0, 6.0, ((0, 32), (1, 2))),
        "first_assign": set_ends(jax.random.randint(key_of[1], (ROWS,), 0, BUCKETS), jax.random.fold_in(key_of[1], 1), 0, BUCKETS - 1).astype(jnp.int32),
        "second_assign": set_ends(jax.random.randint(key_of[2], (ROWS,), 0, BUCKETS), jax.random.fold_in(key_of[2], 1), 0, BUCKETS - 1).astype(jnp.int32),
        "start_centroids": normal_values(key_of[3], (BUCKETS, BINS), 0.5, 3.0, ((0, 4), (1, 2)), jnp.float32),
    }


def lloyd_update(previous, histograms, assign):
    sums = jax.ops.segment_sum(histograms.astype(jnp.float32), assign, num_segments=BUCKETS)
    counts = jax.ops.segment_sum(jnp.ones(assign.shape, jnp.float32), assign, num_segments=BUCKETS)
    return (sums + PRIOR * previous) / (counts + PRIOR)[:, None]


def reference(histograms, first_assign, second_assign, start_centroids):
    middle = lloyd_update(start_centroids, histograms, first_assign)
    centroids = lloyd_update(middle, histograms, second_assign)
    rounded = centroids.astype(jnp.bfloat16)
    norms = jnp.sum(centroids * centroids, axis=1)
    block_rows = ROW_DEV // 2
    blocks = histograms.reshape(ROWS // block_rows, block_rows, BINS)

    def least(block):
        dots = jnp.dot(block, rounded.T, preferred_element_type=jnp.float32)
        return jnp.min(norms[None, :] - 2.0 * dots, axis=1)

    distortion = lax.map(least, blocks).reshape(ROWS)
    return centroids, distortion
```

```python
import jax
import jax.numpy as jnp
from jax import lax
from jax.experimental import pallas as pl
from jax.experimental.pallas import tpu as pltpu
from jax.sharding import PartitionSpec as P

MESH = pl.DeviceIdType.MESH
F32, BF16 = jnp.float32, jnp.bfloat16
NYH, NZ, NCORE = 2, 8, 2
CHIPS = NYH * NZ
PANELS, BINS2 = 4, 2
ROWS, LANES = 12288, 128
PANEL_ROWS = 256
HALF = PANEL_ROWS // NCORE
OWN = HALF // CHIPS
PRIOR = 384.0
PART = ROWS // (PANELS * BINS2)
CHUNK = 1024
NCHUNK = ROWS // CHUNK
TILE = 256

(S_ROWS, S_PART, S_SIB, S_FWD, S_PAIR, S_SUMS, S_CENT, S_COPY, S_PANEL, S_NORM, S_LEAST, N_SEM) = range(12)


def kernel(hist, first, second, start, cent_out, dist_out,
           hv, rows, acc, pair, sib, red, sums, cent, full, norms, norm_col, least, least_all,
           load_sem, send_sem, recv_sem):
    dp, panel, half_bin = lax.axis_index("dp"), lax.axis_index("panel"), lax.axis_index("bin")
    yh, z, core = dp // (NZ * NCORE), lax.rem(dp // NCORE, NZ), lax.rem(dp, NCORE)
    chip = yh * NZ + z
    other = 1 - core
    sib_dp = chip * NCORE + other
    bin_peer = 1 - half_bin

    def device(dp_to, panel_to, bin_to):
        return {"dp": dp_to, "panel": panel_to, "bin": bin_to}

    def chip_at(shift):
        yh_to = lax.rem(yh + shift // NZ, NYH)
        return yh_to * NZ + lax.rem(z + shift % NZ, NZ)

    def panel_at(shift):
        return lax.rem(panel + shift, PANELS)

    def remote(src, dst, sem, to):
        return pltpu.make_async_remote_copy(
            src_ref=src, dst_ref=dst, send_sem=send_sem.at[sem], recv_sem=recv_sem.at[sem],
            device_id=to, device_id_type=MESH)

    def wait(ref, sem):
        pltpu.make_async_copy(ref, ref, sem).wait()

    seven = rows.at[pl.ds(0, 7 * HALF), pl.ds(0, LANES)]
    sibling = device(sib_dp, panel, half_bin)
    shifts = sorted(range(1, CHIPS), key=lambda s: -min(s % NZ, NZ - s % NZ))
    chips = [(s, chip_at(s)) for s in shifts]
    around = [(dx, db) for dx in (2, 1, 3, 0) for db in (1, 0) if dx or db]

    barrier = pltpu.get_barrier_semaphore()
    peers = [sibling]
    peers += [device(q * NCORE + core, panel, half_bin) for _, q in chips]
    peers += [device(dp, panel_at(dx), bin_peer if db else half_bin) for dx, db in around]
    peers += [device(sib_dp, panel_at(dx), half_bin) for dx in (1, 2, 3)]
    for to in peers:
        pl.semaphore_signal(barrier, inc=1, device_id=to, device_id_type=MESH)

    loads = []
    for i in range(NCHUNK):
        at = pl.ds(i * CHUNK, CHUNK)
        load = pltpu.make_async_copy(hist.at[at], hv.at[at, pl.ds(0, LANES)], load_sem.at[i])
        load.start()
    own_part = half_bin * (ROWS // 2) + panel * PART
    peer_part = bin_peer * (ROWS // 2) + panel * PART
    own_rows = pltpu.make_async_copy(
        hist.at[pl.ds(own_part, PART)], rows.at[pl.ds(0, PART), pl.ds(0, LANES)], load_sem.at[NCHUNK])
    own_rows.start()

    hv[:, LANES:] = jnp.ones((ROWS, LANES), BF16)
    acc[...] = jnp.zeros_like(acc)

    pl.semaphore_wait(barrier, len(peers))
    to_peer = remote(hist.at[pl.ds(peer_part, PART)], rows.at[pl.ds(0, PART), pl.ds(LANES, LANES)], S_PART,
                     device(dp, panel, bin_peer))
    to_sib = remote(hist.at[pl.ds(own_part, PART)], rows.at[pl.ds(PART, PART), pl.ds(0, LANES)], S_SIB, sibling)
    to_peer.start()
    to_sib.start()

    with jax.named_scope("local_sums"):
        bucket = lax.broadcasted_iota(jnp.int32, (PANEL_ROWS, LANES), 0).astype(F32).astype(BF16)
        one, zero = jnp.ones((), BF16), jnp.zeros((), BF16)

        def step(i, carry):
            at = pl.ds(pl.multiple_of(i * CHUNK, CHUNK), CHUNK)
            wait(hv.at[at, pl.ds(0, LANES)], load_sem.at[i])
            hots = []
            for assign in (first, second):
                ids = assign[pl.ds(pl.multiple_of(i * 8, 8), 8), :] - panel * PANEL_ROWS
                ids = ids.astype(F32)
                hots.append(jnp.concatenate([
                    jnp.where(jnp.broadcast_to(ids[j:j + 1, :], (PANEL_ROWS, LANES)).astype(BF16) == bucket, one, zero)
                    for j in range(CHUNK // LANES)], axis=1))
            hot = jnp.concatenate(hots, axis=0)
            acc[...] += jnp.dot(hot, hv[at, :], preferred_element_type=F32)
            return carry

        lax.fori_loop(0, NCHUNK, step, 0)

    with jax.named_scope("pair_sums"):
        lane = lax.broadcasted_iota(jnp.int32, (PANEL_ROWS, LANES), 1)
        count = jnp.where(lane < LANES // 2, acc[:PANEL_ROWS, LANES:], acc[PANEL_ROWS:, LANES:])
        groups = (PANEL_ROWS // OWN, OWN, LANES)
        pair[:, 0] = acc[:PANEL_ROWS, :LANES].reshape(groups)
        pair[:, 1] = acc[PANEL_ROWS:, :LANES].reshape(groups)
        pair[:, 2] = count.reshape(groups)
        to_pair = remote(pair.at[pl.ds(other * CHIPS, CHIPS)], sib, S_PAIR, sibling)
        to_pair.start()
        to_pair.wait_recv()
        red[...] = pair[pl.ds(core * CHIPS, CHIPS)] + sib[...]

    with jax.named_scope("chip_sums"):
        for i, (s, q) in enumerate(chips):
            remote(red.at[q], sums.at[i], S_SUMS, device(q * NCORE + core, panel, half_bin)).start()
        wait(sums, recv_sem.at[S_SUMS])
        total = red[chip]
        for i in range(CHIPS - 1):
            total += sums[i]
        here = pl.ds(pl.multiple_of(core * HALF + chip * OWN, OWN), OWN)
        middle = (total[0] + PRIOR * start[here, :]) / (total[2, :, 0:1] + PRIOR)
        cent[here, :] = (total[1] + PRIOR * middle) / (total[2, :, LANES // 2:LANES // 2 + 1] + PRIOR)

    with jax.named_scope("gather_chips"):
        for s, q in chips:
            remote(cent.at[here], cent.at[here], S_CENT, device(q * NCORE + core, panel, half_bin)).start()
        to_peer.wait_recv()
        forward = remote(rows.at[pl.ds(0, PART), pl.ds(LANES, LANES)], rows.at[pl.ds(PART, PART), pl.ds(LANES, LANES)],
                         S_FWD, sibling)
        forward.start()
        wait(cent.at[pl.ds(0, HALF - OWN)], recv_sem.at[S_CENT])

    with jax.named_scope("gather_panels"):
        mine = pl.ds(pl.multiple_of(core * HALF, HALF), HALF)
        to_copy = remote(cent.at[mine], cent.at[mine], S_COPY, sibling)
        value = cent[mine, :]
        full[pl.ds(0, HALF), pl.ds(0, LANES)] = (-2.0 * value).astype(BF16)
        for dx, db in around:
            remote(full.at[pl.ds(0, HALF), pl.ds(0, LANES)],
                   full.at[pl.ds((PANELS - dx) % PANELS * HALF, HALF), pl.ds(db * LANES, LANES)],
                   S_PANEL, device(dp, panel_at(dx), bin_peer if db else half_bin)).start()
        norms[0] = jnp.sum((value * value).T, axis=0, keepdims=True)
        for dx, db in around:
            remote(norms.at[0], norms.at[db * PANELS + (PANELS - dx) % PANELS],
                   S_NORM, device(dp, panel_at(dx), bin_peer if db else half_bin)).start()
        to_copy.start()
        own_rows.wait()
        to_sib.wait_recv()
        forward.wait_recv()
        wait(norms.at[pl.ds(1, 7)], recv_sem.at[S_NORM])
        for j in range(PANELS):
            row = norms[j] + norms[PANELS + j]
            norm_col[pl.ds(j * HALF, HALF), :] = jnp.broadcast_to(row, (HALF, HALF)).T
        wait(seven, recv_sem.at[S_PANEL])

    with jax.named_scope("least"):
        for t in range(2 * PART // TILE):
            dots = lax.dot_general(full[...], rows[pl.ds(t * TILE, TILE), :], (((1,), (1,)), ((), ())),
                                   preferred_element_type=F32)
            col = norm_col[...]
            value = dots + jnp.concatenate([col, col], axis=1)
            at = pl.ds(t * TILE % PART, TILE)
            least[t * TILE // PART, :, at] = jnp.min(value, axis=0, keepdims=True)

    with jax.named_scope("gather_least"):
        for dx in (2, 1, 3):
            remote(least.at[0], least_all.at[panel], S_LEAST, device(dp, panel_at(dx), half_bin)).start()
        for dx in (2, 1, 3, 0):
            remote(least.at[1], least_all.at[PANELS + panel], S_LEAST, device(sib_dp, panel_at(dx), half_bin)).start()
        least_all[panel] = least[0]
        to_copy.wait_recv()
        cent_out[...] = cent[...]
        wait(least_all.at[pl.ds(0, 7)], recv_sem.at[S_LEAST])
        dist_out[...] = jnp.minimum(least_all[pl.ds(0, PANELS)], least_all[pl.ds(PANELS, PANELS)])

    to_peer.wait_send()
    to_sib.wait_send()
    to_pair.wait_send()
    wait(sums, send_sem.at[S_SUMS])
    wait(cent.at[pl.ds(0, HALF - OWN)], send_sem.at[S_CENT])
    forward.wait_send()
    to_copy.wait_send()
    wait(seven, send_sem.at[S_PANEL])
    wait(norms.at[pl.ds(1, 7)], send_sem.at[S_NORM])
    wait(least_all.at[pl.ds(0, 7)], send_sem.at[S_LEAST])


def on_device(histograms, first_assign, second_assign, start_centroids):
    vmem = pl.BlockSpec(memory_space=pltpu.VMEM)
    cent, dist = pl.pallas_call(
        kernel,
        out_shape=(
            jax.ShapeDtypeStruct((PANEL_ROWS, LANES), F32),
            jax.ShapeDtypeStruct((PANELS, 1, PART), F32),
        ),
        in_specs=[pl.BlockSpec(memory_space=pltpu.HBM), vmem, vmem, vmem],
        out_specs=(vmem, vmem),
        scratch_shapes=[
            pltpu.VMEM((ROWS, 2 * LANES), BF16),
            pltpu.VMEM((2 * PART, 2 * LANES), BF16),
            pltpu.VMEM((2 * PANEL_ROWS, 2 * LANES), F32),
            pltpu.VMEM((PANEL_ROWS // OWN, 3, OWN, LANES), F32),
            pltpu.VMEM((CHIPS, 3, OWN, LANES), F32),
            pltpu.VMEM((CHIPS, 3, OWN, LANES), F32),
            pltpu.VMEM((CHIPS - 1, 3, OWN, LANES), F32),
            pltpu.VMEM((PANEL_ROWS, LANES), F32),
            pltpu.VMEM((PANELS * HALF, 2 * LANES), BF16),
            pltpu.VMEM((BINS2 * PANELS, 1, HALF), F32),
            pltpu.VMEM((PANELS * HALF, LANES), F32),
            pltpu.VMEM((2, 1, PART), F32),
            pltpu.VMEM((2 * PANELS, 1, PART), F32),
            pltpu.SemaphoreType.DMA((NCHUNK + 1,)),
            pltpu.SemaphoreType.DMA((N_SEM,)),
            pltpu.SemaphoreType.DMA((N_SEM,)),
        ],
        compiler_params=pltpu.CompilerParams(
            collective_id=0, has_side_effects=True, vmem_limit_bytes=32 * 1024 * 1024),
    )(histograms, first_assign.reshape(ROWS // LANES, LANES), second_assign.reshape(ROWS // LANES, LANES),
      start_centroids)
    return cent, dist.reshape(PANELS * PART)


def solution(mesh):
    return jax.shard_map(
        on_device,
        mesh=mesh,
        in_specs=(P("dp", "bin"), P("dp"), P("dp"), P("panel", "bin")),
        out_specs=(P("panel", "bin"), P(("dp", "bin"))),
        check_vma=False,
    )
```

```python
import jax
import jax.numpy as jnp
from jax import lax
from jax.experimental import pallas as pl
from jax.experimental.pallas import tpu as pltpu
from jax.sharding import PartitionSpec as P

MESH = pl.DeviceIdType.MESH
F32, BF16 = jnp.float32, jnp.bfloat16
NYH, NZ, NCORE = 2, 8, 2
CHIPS = NYH * NZ
PANELS = 4
ROWS, LANES = 12288, 128
OUT_ROWS = ROWS // 2
PANEL_ROWS = 256
HALF = PANEL_ROWS // NCORE
OWN = HALF // CHIPS
PRIOR = 384.0
CHUNKS = (2048, 4096, 6144)
TILE = 256
DIRECT = 1536
QUARTER = (OUT_ROWS - DIRECT) // PANELS
PIECES = 3
PIECE = QUARTER // PIECES

(S_DIRECT, S_ACROSS, S_PAIR, S_SUMS, S_COUNTS, S_CENT, S_COPY, S_LEAST, S_PIECE) = range(9)
N_SEM = S_PIECE + PIECES


def kernel(hist, first_in, second_in, start_in, cent_out, dist_out,
           hv, first, second, start, rows, acc, pair, sib, red, sums, count, counts, cent, full, norm, least,
           load_sem, send_sem, recv_sem):
    dp, panel, half_bin = lax.axis_index("dp"), lax.axis_index("panel"), lax.axis_index("bin")
    yh, z, core = dp // (NZ * NCORE), lax.rem(dp // NCORE, NZ), lax.rem(dp, NCORE)
    chip = yh * NZ + z
    other = 1 - core
    bin_peer = 1 - half_bin

    def device(dp_to, panel_to, bin_to):
        return {"dp": dp_to, "panel": panel_to, "bin": bin_to}

    def chip_at(shift):
        yh_to = lax.rem(yh + shift // NZ, NYH)
        return yh_to * NZ + lax.rem(z + shift % NZ, NZ)

    def remote(src, dst, sem, to):
        return pltpu.make_async_remote_copy(
            src_ref=src, dst_ref=dst, send_sem=send_sem.at[sem], recv_sem=recv_sem.at[sem],
            device_id=to, device_id_type=MESH)

    def wait(ref, sem):
        pltpu.make_async_copy(ref, ref, sem).wait()

    sibling = device(chip * NCORE + other, panel, half_bin)
    across = [device(dp, lax.rem(panel + dx, PANELS), half_bin) for dx in (2, 1, 3)]
    shifts = sorted(range(CHIPS), key=lambda s: -min(s % NZ, NZ - s % NZ) - 2 * (s // NZ))
    chips = [chip_at(s) for s in shifts if s]
    same_bin = [device(q * NCORE + core, panel, half_bin) for q in chips]
    other_bin = [device(chip_at(s) * NCORE + core, panel, bin_peer) for s in shifts]

    barrier = pltpu.get_barrier_semaphore()
    peers = same_bin + other_bin + across + [sibling]
    for to in peers:
        pl.semaphore_signal(barrier, inc=1, device_id=to, device_id_type=MESH)

    small = [pltpu.make_async_copy(src, dst, load_sem.at[i])
             for i, (src, dst) in enumerate(((first_in, first), (second_in, second), (start_in, start)))]
    begins = [sum(CHUNKS[:i]) for i in range(len(CHUNKS))]
    loads = [pltpu.make_async_copy(hist.at[pl.ds(at, n)], hv.at[pl.ds(at, n), pl.ds(0, LANES)], load_sem.at[3 + i])
             for i, (at, n) in enumerate(zip(begins, CHUNKS))]
    own_rows = pltpu.make_async_copy(
        hist.at[pl.ds(half_bin * OUT_ROWS, OUT_ROWS)], rows.at[:, pl.ds(0, LANES)], load_sem.at[3 + len(CHUNKS)])
    for copy in small[:2] + loads + small[2:] + [own_rows]:
        copy.start()

    hv[:, LANES:] = jnp.ones((ROWS, LANES), BF16)

    with jax.named_scope("local_sums"):
        bucket = lax.broadcasted_iota(jnp.int32, (PANEL_ROWS, LANES), 0).astype(F32).astype(BF16)
        one, zero = jnp.ones((), BF16), jnp.zeros((), BF16)
        for copy in small[:2]:
            copy.wait()
        for at, n, load in zip(begins, CHUNKS, loads):
            hots = []
            for assign in (first, second):
                ids = (assign[at // LANES:(at + n) // LANES, :] - panel * PANEL_ROWS).astype(F32)
                hots.append(jnp.concatenate([
                    jnp.where(jnp.broadcast_to(ids[j:j + 1, :], (PANEL_ROWS, LANES)).astype(BF16) == bucket, one, zero)
                    for j in range(n // LANES)], axis=1))
            hot = jnp.concatenate(hots, axis=0)
            load.wait()
            part = jnp.dot(hot, hv[at:at + n, :], preferred_element_type=F32)
            if at:
                acc[...] += part
            else:
                acc[...] = part

    pl.semaphore_wait(barrier, len(peers))

    with jax.named_scope("pair_sums"):
        lane = lax.broadcasted_iota(jnp.int32, (PANEL_ROWS, LANES), 1)
        both = jnp.where(lane < LANES // 2, acc[:PANEL_ROWS, LANES:], acc[PANEL_ROWS:, LANES:])
        groups = (PANEL_ROWS // OWN, OWN, LANES)
        pair[:, 0] = acc[:PANEL_ROWS, :LANES].reshape(groups)
        pair[:, 1] = acc[PANEL_ROWS:, :LANES].reshape(groups)
        pair[:, 2] = both.reshape(groups)
        to_pair = remote(pair.at[pl.ds(other * CHIPS, CHIPS)], sib, S_PAIR, sibling)
        to_pair.start()

        base = bin_peer * OUT_ROWS
        peer = device(dp, panel, bin_peer)
        quarter = DIRECT + panel * QUARTER
        pieces = [remote(hist.at[pl.ds(base + quarter + i * PIECE, PIECE)],
                         rows.at[pl.ds(quarter + i * PIECE, PIECE), pl.ds(LANES, LANES)], S_PIECE + i, peer)
                  for i in range(PIECES)]
        direct = remote(hist.at[pl.ds(base, DIRECT)], rows.at[pl.ds(0, DIRECT), pl.ds(LANES, LANES)], S_DIRECT, peer)
        for copy in pieces + [direct]:
            copy.start()

        to_pair.wait_recv()
        own = pl.ds(core * CHIPS, CHIPS)
        red[...] = pair[own, 0:2] + sib[:, 0:2]
        turned = (pair[own, 2] + sib[:, 2]).reshape(HALF, LANES).T
        count[0] = turned[0:1, :]
        count[1] = turned[LANES // 2:LANES // 2 + 1, :]

    with jax.named_scope("chip_sums"):
        for i, (q, to) in enumerate(zip(chips, same_bin)):
            remote(red.at[q], sums.at[i], S_SUMS, to).start()
            remote(count, counts.at[i], S_COUNTS, to).start()
        for i, copy in enumerate(pieces):
            copy.wait_recv()
            at = rows.at[pl.ds(quarter + i * PIECE, PIECE), pl.ds(LANES, LANES)]
            for to in across:
                remote(at, at, S_ACROSS, to).start()
        for copy in small[2:]:
            copy.wait()
        wait(counts, recv_sem.at[S_COUNTS])
        number = count[...]
        for i in range(CHIPS - 1):
            number += counts[i]
        mark = (lax.broadcasted_iota(jnp.int32, (OWN, LANES), 1)
                == lax.broadcasted_iota(jnp.int32, (OWN, LANES), 0) + chip * OWN)
        weight = [jnp.sum(jnp.where(mark, jnp.broadcast_to(number[s], (OWN, LANES)), 0.0), axis=1, keepdims=True) + PRIOR
                  for s in range(2)]
        here = pl.ds(pl.multiple_of(core * HALF + chip * OWN, OWN), OWN)
        before = PRIOR * start[here, :]
        wait(sums, recv_sem.at[S_SUMS])
        total = red[chip]
        for i in range(CHIPS - 1):
            total += sums[i]
        middle = (total[0] + before) / weight[0]
        cent[0, here, :] = (total[1] + PRIOR * middle) / weight[1]

    with jax.named_scope("gather_chips"):
        for i in range(CHIPS):
            remote(cent.at[0, here], cent.at[1, here], S_CENT, other_bin[i]).start()
            if i < CHIPS - 1:
                remote(cent.at[0, here], cent.at[0, here], S_CENT, same_bin[i]).start()
        slices = acc.at[pl.ds(0, 2 * HALF - OWN), pl.ds(0, LANES)]
        wait(slices, recv_sem.at[S_CENT])

    with jax.named_scope("gather_cores"):
        mine = pl.ds(pl.multiple_of(core * HALF, HALF), HALF)
        theirs = pl.ds(pl.multiple_of(other * HALF, HALF), HALF)
        to_copy = remote(cent.at[:, mine], cent.at[:, mine], S_COPY, sibling)
        to_copy.start()

        def prepare(at, buckets):
            value = jnp.concatenate([cent[0, at, :], cent[1, at, :]], axis=1)
            full[buckets, :] = (-2.0 * value).astype(BF16)
            norm[buckets, :] = jnp.broadcast_to(jnp.sum(value * value, axis=1, keepdims=True), (HALF, LANES))

        prepare(mine, slice(0, HALF))
        own_rows.wait()
        to_copy.wait_recv()
        prepare(theirs, slice(HALF, PANEL_ROWS))
        direct.wait_recv()
        wait(rows.at[pl.ds(0, (PANELS - 1) * QUARTER), pl.ds(LANES, LANES)], recv_sem.at[S_ACROSS])

    with jax.named_scope("least"):
        for t in range(OUT_ROWS // TILE):
            dots = lax.dot_general(full[...], rows[t * TILE:(t + 1) * TILE, :], (((1,), (1,)), ((), ())),
                                   preferred_element_type=F32)
            value = dots + jnp.concatenate([norm[...]] * (TILE // LANES), axis=1)
            least[0, :, t * TILE:(t + 1) * TILE] = jnp.min(value, axis=0, keepdims=True)
            if (t + 1) * TILE in (OUT_ROWS // 2, OUT_ROWS):
                part = pl.ds((t + 1) * TILE - OUT_ROWS // 2, OUT_ROWS // 2)
                for dx, to in zip((2, 1, 3), across):
                    remote(least.at[0, :, part], least.at[dx, :, part], S_LEAST, to).start()
        cent_out[...] = cent[0]
        wait(least.at[pl.ds(1, PANELS - 1)], recv_sem.at[S_LEAST])
        dist_out[...] = jnp.minimum(jnp.minimum(least[0], least[1]), jnp.minimum(least[2], least[3]))

    to_pair.wait_send()
    for copy in pieces + [direct]:
        copy.wait_send()
    wait(sums, send_sem.at[S_SUMS])
    wait(counts, send_sem.at[S_COUNTS])
    wait(rows.at[pl.ds(0, (PANELS - 1) * QUARTER), pl.ds(LANES, LANES)], send_sem.at[S_ACROSS])
    wait(slices, send_sem.at[S_CENT])
    to_copy.wait_send()
    wait(least.at[pl.ds(1, PANELS - 1)], send_sem.at[S_LEAST])


def on_device(histograms, first_assign, second_assign, start_centroids):
    vmem = pl.BlockSpec(memory_space=pltpu.VMEM)
    args = [pltpu.with_memory_space_constraint(a, pltpu.HBM) for a in (
        histograms, first_assign.reshape(ROWS // LANES, LANES), second_assign.reshape(ROWS // LANES, LANES),
        start_centroids)]
    cent, dist = pl.pallas_call(
        kernel,
        out_shape=(pltpu.VMEM((PANEL_ROWS, LANES), F32), pltpu.VMEM((1, OUT_ROWS), F32)),
        in_specs=[pl.BlockSpec(memory_space=pltpu.HBM)] * 4,
        out_specs=(vmem, vmem),
        scratch_shapes=[
            pltpu.VMEM((ROWS, 2 * LANES), BF16),
            pltpu.VMEM((ROWS // LANES, LANES), jnp.int32),
            pltpu.VMEM((ROWS // LANES, LANES), jnp.int32),
            pltpu.VMEM((PANEL_ROWS, LANES), F32),
            pltpu.VMEM((OUT_ROWS, 2 * LANES), BF16),
            pltpu.VMEM((2 * PANEL_ROWS, 2 * LANES), F32),
            pltpu.VMEM((PANEL_ROWS // OWN, 3, OWN, LANES), F32),
            pltpu.VMEM((CHIPS, 3, OWN, LANES), F32),
            pltpu.VMEM((CHIPS, 2, OWN, LANES), F32),
            pltpu.VMEM((CHIPS - 1, 2, OWN, LANES), F32),
            pltpu.VMEM((2, 1, LANES), F32),
            pltpu.VMEM((CHIPS - 1, 2, 1, LANES), F32),
            pltpu.VMEM((2, PANEL_ROWS, LANES), F32),
            pltpu.VMEM((PANEL_ROWS, 2 * LANES), BF16),
            pltpu.VMEM((PANEL_ROWS, LANES), F32),
            pltpu.VMEM((PANELS, 1, OUT_ROWS), F32),
            pltpu.SemaphoreType.DMA((len(CHUNKS) + 4,)),
            pltpu.SemaphoreType.DMA((N_SEM,)),
            pltpu.SemaphoreType.DMA((N_SEM,)),
        ],
        compiler_params=pltpu.CompilerParams(
            collective_id=0, has_side_effects=True, vmem_limit_bytes=48 * 1024 * 1024),
    )(*args)
    return cent, dist.reshape(OUT_ROWS)


def solution(mesh):
    return jax.shard_map(
        on_device,
        mesh=mesh,
        in_specs=(P("dp", "bin"), P("dp"), P("dp"), P("panel", "bin")),
        out_specs=(P("panel", "bin"), P(("dp", "bin"))),
        check_vma=False,
    )
```

```python
import jax
import jax.numpy as jnp
from jax import lax
from jax.experimental import pallas as pl
from jax.experimental.pallas import tpu as pltpu
from jax.sharding import PartitionSpec as P

MESH = pl.DeviceIdType.MESH
F32, BF16 = jnp.float32, jnp.bfloat16
NYH, NZ, NCORE = 2, 8, 2
CHIPS = NYH * NZ
PANELS = 4
ROWS, LANES = 12288, 128
OUT_ROWS = ROWS // 2
PANEL_ROWS = 256
HALF = PANEL_ROWS // NCORE
OWN = HALF // CHIPS
PRIOR = 384.0
CHUNKS = (2048, 4096, 6144)
TILE = 256
QUARTER = OUT_ROWS // PANELS
PIECES = 4
EARLY = 4
PIECE = QUARTER // PIECES

(S_ACROSS, S_PAIR, S_SUMS, S_COUNTS, S_CENT, S_COPY, S_LEAST, S_PIECE) = range(8)
N_SEM = S_PIECE + PIECES


def kernel(hist, first_in, second_in, start_in, cent_out, dist_out,
           hv, first, second, start, rows, acc, pair, sib, red, sums, count, counts, cent, full, norm, least,
           load_sem, send_sem, recv_sem, near_sem, far_sem):
    dp, panel, half_bin = lax.axis_index("dp"), lax.axis_index("panel"), lax.axis_index("bin")
    yh, z, core = dp // (NZ * NCORE), lax.rem(dp // NCORE, NZ), lax.rem(dp, NCORE)
    chip = yh * NZ + z
    other = 1 - core
    bin_peer = 1 - half_bin

    def device(dp_to, panel_to, bin_to):
        return {"dp": dp_to, "panel": panel_to, "bin": bin_to}

    def chip_at(shift):
        yh_to = lax.rem(yh + shift // NZ, NYH)
        return yh_to * NZ + lax.rem(z + shift % NZ, NZ)

    def remote(src, dst, sem, to):
        return pltpu.make_async_remote_copy(
            src_ref=src, dst_ref=dst, send_sem=send_sem.at[sem], recv_sem=recv_sem.at[sem],
            device_id=to, device_id_type=MESH)

    def wait(ref, sem):
        pltpu.make_async_copy(ref, ref, sem).wait()

    sibling = device(chip * NCORE + other, panel, half_bin)
    across = [device(dp, lax.rem(panel + dx, PANELS), half_bin) for dx in (2, 1, 3)]
    shifts = sorted(range(CHIPS), key=lambda s: -min(s % NZ, NZ - s % NZ) - 2 * (s // NZ))
    chips = [chip_at(s) for s in shifts if s]
    same_bin = [device(q * NCORE + core, panel, half_bin) for q in chips]
    other_bin = [device(chip_at(s) * NCORE + core, panel, bin_peer) for s in shifts]

    barrier = pltpu.get_barrier_semaphore()
    near = [other_bin[-1]] + across
    far = same_bin + other_bin[:-1]

    def signal(semaphore, to):
        pl.semaphore_signal(semaphore, inc=1, device_id=to, device_id_type=MESH)

    for to in near:
        signal(barrier, device(chip * NCORE, to["panel"], to["bin"]))
    signal(barrier, sibling)
    for to in far:
        signal(barrier, device(to["dp"] - core + 1, to["panel"], to["bin"]))

    def wait_near():
        @pl.when(core == 0)
        def _():
            pl.semaphore_wait(barrier, NCORE * len(near) + 1)
            signal(near_sem, sibling)

        @pl.when(core == 1)
        def _():
            pl.semaphore_wait(near_sem, 1)

    def wait_far():
        @pl.when(core == 1)
        def _():
            pl.semaphore_wait(barrier, NCORE * len(far) + 1)
            signal(far_sem, sibling)

        @pl.when(core == 0)
        def _():
            pl.semaphore_wait(far_sem, 1)

    base = bin_peer * OUT_ROWS
    quarter = panel * QUARTER
    pieces = [remote(hist.at[pl.ds(base + quarter + i * PIECE, PIECE)],
                     rows.at[pl.ds(quarter + i * PIECE, PIECE), pl.ds(LANES, LANES)], S_PIECE + i, other_bin[-1])
              for i in range(PIECES)]

    def send_pieces():
        for copy in pieces:
            copy.start()

    def pass_on(which):
        for i in which:
            pieces[i].wait_recv()
            at = rows.at[pl.ds(quarter + i * PIECE, PIECE), pl.ds(LANES, LANES)]
            for to in across:
                remote(at, at, S_ACROSS, to).start()

    early = z < EARLY

    small = [pltpu.make_async_copy(src, dst, load_sem.at[i])
             for i, (src, dst) in enumerate(((first_in, first), (second_in, second), (start_in, start)))]
    begins = [sum(CHUNKS[:i]) for i in range(len(CHUNKS))]
    loads = [pltpu.make_async_copy(hist.at[pl.ds(at, n)], hv.at[pl.ds(at, n), pl.ds(0, LANES)], load_sem.at[3 + i])
             for i, (at, n) in enumerate(zip(begins, CHUNKS))]
    own_rows = pltpu.make_async_copy(
        hist.at[pl.ds(half_bin * OUT_ROWS, OUT_ROWS)], rows.at[:, pl.ds(0, LANES)], load_sem.at[3 + len(CHUNKS)])
    for copy in small[:2] + loads + small[2:] + [own_rows]:
        copy.start()

    hv[:, LANES:] = jnp.ones((ROWS, LANES), BF16)

    @pl.when(early)
    def _():
        wait_near()
        send_pieces()

    with jax.named_scope("local_sums"):
        bucket = lax.broadcasted_iota(jnp.int32, (PANEL_ROWS, LANES), 0).astype(F32).astype(BF16)
        one, zero = jnp.ones((), BF16), jnp.zeros((), BF16)
        for copy in small[:2]:
            copy.wait()
        for at, n, load in zip(begins, CHUNKS, loads):
            hots = []
            for assign in (first, second):
                ids = (assign[at // LANES:(at + n) // LANES, :] - panel * PANEL_ROWS).astype(F32)
                hots.append(jnp.concatenate([
                    jnp.where(jnp.broadcast_to(ids[j:j + 1, :], (PANEL_ROWS, LANES)).astype(BF16) == bucket, one, zero)
                    for j in range(n // LANES)], axis=1))
            hot = jnp.concatenate(hots, axis=0)
            load.wait()
            part = jnp.dot(hot, hv[at:at + n, :], preferred_element_type=F32)
            if at:
                acc[...] += part
            else:
                acc[...] = part

    @pl.when(early)
    def _():
        pass_on(range(PIECES))

    @pl.when(jnp.logical_not(early))
    def _():
        wait_near()

    wait_far()

    with jax.named_scope("pair_sums"):
        lane = lax.broadcasted_iota(jnp.int32, (PANEL_ROWS, LANES), 1)
        both = jnp.where(lane < LANES // 2, acc[:PANEL_ROWS, LANES:], acc[PANEL_ROWS:, LANES:])
        groups = (PANEL_ROWS // OWN, OWN, LANES)
        pair[:, 0] = acc[:PANEL_ROWS, :LANES].reshape(groups)
        pair[:, 1] = acc[PANEL_ROWS:, :LANES].reshape(groups)
        pair[:, 2] = both.reshape(groups)
        to_pair = remote(pair.at[pl.ds(other * CHIPS, CHIPS)], sib, S_PAIR, sibling)
        to_pair.start()

        to_pair.wait_recv()
        own = pl.ds(core * CHIPS, CHIPS)
        red[...] = pair[own, 0:2] + sib[:, 0:2]
        turned = (pair[own, 2] + sib[:, 2]).reshape(HALF, LANES).T
        count[0] = turned[0:1, :]
        count[1] = turned[LANES // 2:LANES // 2 + 1, :]

    with jax.named_scope("chip_sums"):
        for i, (q, to) in enumerate(zip(chips, same_bin)):
            remote(red.at[q], sums.at[i], S_SUMS, to).start()
            remote(count, counts.at[i], S_COUNTS, to).start()

        @pl.when(jnp.logical_not(early))
        def _():
            send_pieces()
            pass_on(range(PIECES // 2))

        for copy in small[2:]:
            copy.wait()
        wait(counts, recv_sem.at[S_COUNTS])
        number = count[...]
        for i in range(CHIPS - 1):
            number += counts[i]
        mark = (lax.broadcasted_iota(jnp.int32, (OWN, LANES), 1)
                == lax.broadcasted_iota(jnp.int32, (OWN, LANES), 0) + chip * OWN)
        weight = [jnp.sum(jnp.where(mark, jnp.broadcast_to(number[s], (OWN, LANES)), 0.0), axis=1, keepdims=True) + PRIOR
                  for s in range(2)]
        here = pl.ds(pl.multiple_of(core * HALF + chip * OWN, OWN), OWN)
        before = PRIOR * start[here, :]
        wait(sums, recv_sem.at[S_SUMS])
        total = red[chip]
        for i in range(CHIPS - 1):
            total += sums[i]
        middle = (total[0] + before) / weight[0]
        cent[0, here, :] = (total[1] + PRIOR * middle) / weight[1]

    with jax.named_scope("gather_chips"):
        for i in range(CHIPS):
            remote(cent.at[0, here], cent.at[1, here], S_CENT, other_bin[i]).start()
            if i < CHIPS - 1:
                remote(cent.at[0, here], cent.at[0, here], S_CENT, same_bin[i]).start()

        @pl.when(jnp.logical_not(early))
        def _():
            pass_on(range(PIECES // 2, PIECES))

        slices = acc.at[pl.ds(0, 2 * HALF - OWN), pl.ds(0, LANES)]
        wait(slices, recv_sem.at[S_CENT])

    with jax.named_scope("gather_cores"):
        mine = pl.ds(pl.multiple_of(core * HALF, HALF), HALF)
        theirs = pl.ds(pl.multiple_of(other * HALF, HALF), HALF)
        to_copy = remote(cent.at[:, mine], cent.at[:, mine], S_COPY, sibling)
        to_copy.start()

        def prepare(at, buckets):
            value = jnp.concatenate([cent[0, at, :], cent[1, at, :]], axis=1)
            full[buckets, :] = (-2.0 * value).astype(BF16)
            norm[buckets, :] = jnp.broadcast_to(jnp.sum(value * value, axis=1, keepdims=True), (HALF, LANES))

        prepare(mine, slice(0, HALF))
        own_rows.wait()
        to_copy.wait_recv()
        prepare(theirs, slice(HALF, PANEL_ROWS))
        wait(rows.at[pl.ds(0, (PANELS - 1) * QUARTER), pl.ds(LANES, LANES)], recv_sem.at[S_ACROSS])

    with jax.named_scope("least"):
        for t in range(OUT_ROWS // TILE):
            dots = lax.dot_general(full[...], rows[t * TILE:(t + 1) * TILE, :], (((1,), (1,)), ((), ())),
                                   preferred_element_type=F32)
            value = dots + jnp.concatenate([norm[...]] * (TILE // LANES), axis=1)
            least[0, :, t * TILE:(t + 1) * TILE] = jnp.min(value, axis=0, keepdims=True)
            if (t + 1) * TILE in (OUT_ROWS // 2, OUT_ROWS):
                part = pl.ds((t + 1) * TILE - OUT_ROWS // 2, OUT_ROWS // 2)
                for dx, to in zip((2, 1, 3), across):
                    remote(least.at[0, :, part], least.at[dx, :, part], S_LEAST, to).start()
        cent_out[...] = cent[0]
        wait(least.at[pl.ds(1, PANELS - 1)], recv_sem.at[S_LEAST])
        dist_out[...] = jnp.minimum(jnp.minimum(least[0], least[1]), jnp.minimum(least[2], least[3]))

    to_pair.wait_send()
    for copy in pieces:
        copy.wait_send()
    wait(sums, send_sem.at[S_SUMS])
    wait(counts, send_sem.at[S_COUNTS])
    wait(rows.at[pl.ds(0, (PANELS - 1) * QUARTER), pl.ds(LANES, LANES)], send_sem.at[S_ACROSS])
    wait(slices, send_sem.at[S_CENT])
    to_copy.wait_send()
    wait(least.at[pl.ds(1, PANELS - 1)], send_sem.at[S_LEAST])


def on_device(histograms, first_assign, second_assign, start_centroids):
    vmem = pl.BlockSpec(memory_space=pltpu.VMEM)
    args = [pltpu.with_memory_space_constraint(a, pltpu.HBM) for a in (
        histograms, first_assign.reshape(ROWS // LANES, LANES), second_assign.reshape(ROWS // LANES, LANES),
        start_centroids)]
    cent, dist = pl.pallas_call(
        kernel,
        out_shape=(pltpu.VMEM((PANEL_ROWS, LANES), F32), pltpu.VMEM((1, OUT_ROWS), F32)),
        in_specs=[pl.BlockSpec(memory_space=pltpu.HBM)] * 4,
        out_specs=(vmem, vmem),
        scratch_shapes=[
            pltpu.VMEM((ROWS, 2 * LANES), BF16),
            pltpu.VMEM((ROWS // LANES, LANES), jnp.int32),
            pltpu.VMEM((ROWS // LANES, LANES), jnp.int32),
            pltpu.VMEM((PANEL_ROWS, LANES), F32),
            pltpu.VMEM((OUT_ROWS, 2 * LANES), BF16),
            pltpu.VMEM((2 * PANEL_ROWS, 2 * LANES), F32),
            pltpu.VMEM((PANEL_ROWS // OWN, 3, OWN, LANES), F32),
            pltpu.VMEM((CHIPS, 3, OWN, LANES), F32),
            pltpu.VMEM((CHIPS, 2, OWN, LANES), F32),
            pltpu.VMEM((CHIPS - 1, 2, OWN, LANES), F32),
            pltpu.VMEM((2, 1, LANES), F32),
            pltpu.VMEM((CHIPS - 1, 2, 1, LANES), F32),
            pltpu.VMEM((2, PANEL_ROWS, LANES), F32),
            pltpu.VMEM((PANEL_ROWS, 2 * LANES), BF16),
            pltpu.VMEM((PANEL_ROWS, LANES), F32),
            pltpu.VMEM((PANELS, 1, OUT_ROWS), F32),
            pltpu.SemaphoreType.DMA((len(CHUNKS) + 4,)),
            pltpu.SemaphoreType.DMA((N_SEM,)),
            pltpu.SemaphoreType.DMA((N_SEM,)),
            pltpu.SemaphoreType.REGULAR,
            pltpu.SemaphoreType.REGULAR,
        ],
        compiler_params=pltpu.CompilerParams(
            collective_id=0, has_side_effects=True, vmem_limit_bytes=48 * 1024 * 1024),
    )(*args)
    return cent, dist.reshape(OUT_ROWS)


def solution(mesh):
    return jax.shard_map(
        on_device,
        mesh=mesh,
        in_specs=(P("dp", "bin"), P("dp"), P("dp"), P("panel", "bin")),
        out_specs=(P("panel", "bin"), P(("dp", "bin"))),
        check_vma=False,
    )
```

```python
import jax
import jax.numpy as jnp
from jax import lax
from jax.experimental import pallas as pl
from jax.experimental.pallas import tpu as pltpu
from jax.sharding import PartitionSpec as P

MESH = pl.DeviceIdType.MESH
F32, BF16 = jnp.float32, jnp.bfloat16
NYH, NZ, NCORE = 2, 8, 2
CHIPS = NYH * NZ
PANELS = 4
ROWS, LANES = 12288, 128
OUT_ROWS = ROWS // 2
PANEL_ROWS = 256
HALF = PANEL_ROWS // NCORE
OWN = HALF // CHIPS
PRIOR = 384.0
CHUNKS = (2048, 6144, 4096)
TILE = 256
QUARTER = OUT_ROWS // PANELS
PIECES = 4
SOON, MID = 2, 4
PIECE = QUARTER // PIECES

S_PAIR, S_SUMS, S_ACROSS, S_COUNTS, S_CENT, S_COPY, S_LEAST, S_PIECE = 0, 2, 4, 5, 6, 7, 8, 9
N_SEM = S_PIECE + PIECES


def kernel(hist, first_in, second_in, start_in, cent_out, dist_out,
           hv, first, second, start, rows, acc, sib, red, sums, count, counts, cent, full, norm, least,
           load_sem, send_sem, recv_sem, near_sem, far_sem):
    dp, panel, half_bin = lax.axis_index("dp"), lax.axis_index("panel"), lax.axis_index("bin")
    yh, z, core = dp // (NZ * NCORE), lax.rem(dp // NCORE, NZ), lax.rem(dp, NCORE)
    chip = yh * NZ + z
    other = 1 - core
    bin_peer = 1 - half_bin

    def device(dp_to, panel_to, bin_to):
        return {"dp": dp_to, "panel": panel_to, "bin": bin_to}

    def chip_at(shift):
        yh_to = lax.rem(yh + shift // NZ, NYH)
        return yh_to * NZ + lax.rem(z + shift % NZ, NZ)

    def remote(src, dst, sem, to):
        return pltpu.make_async_remote_copy(
            src_ref=src, dst_ref=dst, send_sem=send_sem.at[sem], recv_sem=recv_sem.at[sem],
            device_id=to, device_id_type=MESH)

    def wait(ref, sem):
        pltpu.make_async_copy(ref, ref, sem).wait()

    sibling = device(chip * NCORE + other, panel, half_bin)
    across = [device(dp, lax.rem(panel + dx, PANELS), half_bin) for dx in (2, 1, 3)]
    shifts = sorted(range(CHIPS), key=lambda s: -min(s % NZ, NZ - s % NZ) - 2 * (s // NZ))
    chips = [chip_at(s) for s in shifts if s]
    same_bin = [device(q * NCORE + core, panel, half_bin) for q in chips]
    other_bin = [device(chip_at(s) * NCORE + core, panel, bin_peer) for s in shifts]

    small = [pltpu.make_async_copy(src, dst, load_sem.at[i])
             for i, (src, dst) in enumerate(((first_in, first), (second_in, second), (start_in, start)))]
    begins = [sum(CHUNKS[:i]) for i in range(len(CHUNKS))]
    loads = [pltpu.make_async_copy(hist.at[pl.ds(at, n)], hv.at[pl.ds(at, n), pl.ds(0, LANES)], load_sem.at[3 + i])
             for i, (at, n) in enumerate(zip(begins, CHUNKS))]
    own_rows = pltpu.make_async_copy(
        hist.at[pl.ds(half_bin * OUT_ROWS, OUT_ROWS)], rows.at[:, pl.ds(0, LANES)], load_sem.at[3 + len(CHUNKS)])
    for copy in small[:2] + loads + small[2:] + [own_rows]:
        copy.start()

    barrier = pltpu.get_barrier_semaphore()
    near = [other_bin[-1]] + across
    far = same_bin + other_bin[:-1]

    def signal(semaphore, to):
        pl.semaphore_signal(semaphore, inc=1, device_id=to, device_id_type=MESH)

    for to in near:
        signal(barrier, device(chip * NCORE, to["panel"], to["bin"]))
    signal(barrier, sibling)
    for to in far:
        signal(barrier, device(to["dp"] - core + 1, to["panel"], to["bin"]))

    def wait_near():
        @pl.when(core == 0)
        def _():
            pl.semaphore_wait(barrier, NCORE * len(near) + 1)
            signal(near_sem, sibling)

        @pl.when(core == 1)
        def _():
            pl.semaphore_wait(near_sem, 1)

    def wait_far():
        @pl.when(core == 1)
        def _():
            pl.semaphore_wait(barrier, NCORE * len(far) + 1)
            signal(far_sem, sibling)

        @pl.when(core == 0)
        def _():
            pl.semaphore_wait(far_sem, 1)

    to_pair = [remote(acc.at[s, pl.ds(pl.multiple_of(other * HALF, HALF), HALF)], sib.at[s], S_PAIR + s, sibling)
               for s in range(2)]

    base = bin_peer * OUT_ROWS
    quarter = panel * QUARTER
    pieces = [remote(hist.at[pl.ds(base + quarter + i * PIECE, PIECE)],
                     rows.at[pl.ds(quarter + i * PIECE, PIECE), pl.ds(LANES, LANES)], S_PIECE + i, other_bin[-1])
              for i in range(PIECES)]

    def send_pieces(which):
        for i in which:
            pieces[i].start()

    def pass_on(which):
        for i in which:
            pieces[i].wait_recv()
            at = rows.at[pl.ds(quarter + i * PIECE, PIECE), pl.ds(LANES, LANES)]
            for to in across:
                remote(at, at, S_ACROSS, to).start()

    soon, late = z < SOON, z >= MID
    between = jnp.logical_and(z >= SOON, z < MID)
    half_of = range(PIECES // 2), range(PIECES // 2, PIECES)

    hv[:, LANES:] = jnp.ones((ROWS, LANES), BF16)

    @pl.when(jnp.logical_not(late))
    def _():
        wait_near()
        send_pieces(range(PIECES))

    with jax.named_scope("local_sums"):
        bucket = lax.broadcasted_iota(jnp.int32, (PANEL_ROWS, LANES), 0).astype(F32).astype(BF16)
        one, zero = jnp.ones((), BF16), jnp.zeros((), BF16)
        for copy in small[:2]:
            copy.wait()
        for at, n, load in zip(begins, CHUNKS, loads):
            for s, assign in enumerate((first, second)):
                ids = (assign[at // LANES:(at + n) // LANES, :] - panel * PANEL_ROWS).astype(F32)
                hot = jnp.concatenate([
                    jnp.where(jnp.broadcast_to(ids[j:j + 1, :], (PANEL_ROWS, LANES)).astype(BF16) == bucket, one, zero)
                    for j in range(n // LANES)], axis=1)
                if s == 0:
                    load.wait()
                part = jnp.dot(hot, hv[at:at + n, :], preferred_element_type=F32)
                acc[s] = acc[s] + part if at else part
                if at == begins[-1]:
                    to_pair[s].start()
            if at == begins[0]:
                @pl.when(late)
                def _():
                    wait_near()
                    send_pieces(half_of[0])

    @pl.when(soon)
    def _():
        pass_on(range(PIECES))

    @pl.when(between)
    def _():
        pass_on(half_of[0])

    wait_far()

    with jax.named_scope("chip_sums"):
        own = pl.ds(pl.multiple_of(core * HALF, HALF), HALF)
        diagonal = (lax.broadcasted_iota(jnp.int32, (HALF, LANES), 0)
                    == lax.broadcasted_iota(jnp.int32, (HALF, LANES), 1))
        for s in range(2):
            to_pair[s].wait_recv()
            red[s] = (acc[s, own, :LANES] + sib[s, :, :LANES]).reshape(CHIPS, OWN, LANES)
            count[s] = jnp.sum(jnp.where(diagonal, acc[s, own, LANES:] + sib[s, :, LANES:], 0.0), axis=0, keepdims=True)
            for i, (q, to) in enumerate(zip(chips, same_bin)):
                remote(red.at[s, q], sums.at[s, i], S_SUMS + s, to).start()
                if s:
                    remote(count, counts.at[i], S_COUNTS, to).start()

        @pl.when(late)
        def _():
            send_pieces(half_of[1])
            pass_on(half_of[0])

        @pl.when(jnp.logical_not(soon))
        def _():
            pass_on(half_of[1])

        for copy in small[2:]:
            copy.wait()
        wait(counts, recv_sem.at[S_COUNTS])
        number = count[...]
        for i in range(CHIPS - 1):
            number += counts[i]
        mark = (lax.broadcasted_iota(jnp.int32, (OWN, LANES), 1)
                == lax.broadcasted_iota(jnp.int32, (OWN, LANES), 0) + chip * OWN)
        weight = [jnp.sum(jnp.where(mark, jnp.broadcast_to(number[s], (OWN, LANES)), 0.0), axis=1, keepdims=True) + PRIOR
                  for s in range(2)]
        here = pl.ds(pl.multiple_of(core * HALF + chip * OWN, OWN), OWN)
        before = PRIOR * start[here, :]
        wait(sums.at[0], recv_sem.at[S_SUMS])
        total = red[0, chip]
        for i in range(CHIPS - 1):
            total += sums[0, i]
        middle = (total + before) / weight[0]
        wait(sums.at[1], recv_sem.at[S_SUMS + 1])
        total = red[1, chip]
        for i in range(CHIPS - 1):
            total += sums[1, i]
        cent[0, here, :] = (total + PRIOR * middle) / weight[1]

    with jax.named_scope("gather_chips"):
        for i in range(CHIPS):
            remote(cent.at[0, here], cent.at[1, here], S_CENT, other_bin[i]).start()
            if i < CHIPS - 1:
                remote(cent.at[0, here], cent.at[0, here], S_CENT, same_bin[i]).start()
        slices = acc.at[0, pl.ds(0, 2 * HALF - OWN), pl.ds(0, LANES)]
        wait(slices, recv_sem.at[S_CENT])

    with jax.named_scope("gather_cores"):
        mine = pl.ds(pl.multiple_of(core * HALF, HALF), HALF)
        theirs = pl.ds(pl.multiple_of(other * HALF, HALF), HALF)
        to_copy = remote(cent.at[:, mine], cent.at[:, mine], S_COPY, sibling)
        to_copy.start()

        def prepare(at, buckets):
            value = jnp.concatenate([cent[0, at, :], cent[1, at, :]], axis=1)
            full[buckets, :] = (-2.0 * value).astype(BF16)
            norm[buckets, :] = jnp.broadcast_to(jnp.sum(value * value, axis=1, keepdims=True), (HALF, LANES))

        prepare(mine, slice(0, HALF))
        own_rows.wait()
        to_copy.wait_recv()
        prepare(theirs, slice(HALF, PANEL_ROWS))
        wait(rows.at[pl.ds(0, (PANELS - 1) * QUARTER), pl.ds(LANES, LANES)], recv_sem.at[S_ACROSS])

    with jax.named_scope("least"):
        for t in range(OUT_ROWS // TILE):
            dots = lax.dot_general(full[...], rows[t * TILE:(t + 1) * TILE, :], (((1,), (1,)), ((), ())),
                                   preferred_element_type=F32)
            value = dots + jnp.concatenate([norm[...]] * (TILE // LANES), axis=1)
            least[0, :, t * TILE:(t + 1) * TILE] = jnp.min(value, axis=0, keepdims=True)
            if (t + 1) * TILE in (OUT_ROWS // 2, OUT_ROWS):
                part = pl.ds((t + 1) * TILE - OUT_ROWS // 2, OUT_ROWS // 2)
                for dx, to in zip((2, 1, 3), across):
                    remote(least.at[0, :, part], least.at[dx, :, part], S_LEAST, to).start()
        cent_out[...] = cent[0]
        wait(least.at[pl.ds(1, PANELS - 1)], recv_sem.at[S_LEAST])
        dist_out[...] = jnp.minimum(jnp.minimum(least[0], least[1]), jnp.minimum(least[2], least[3]))

    for copy in to_pair:
        copy.wait_send()
    for copy in pieces:
        copy.wait_send()
    for s in range(2):
        wait(sums.at[s], send_sem.at[S_SUMS + s])
    wait(counts, send_sem.at[S_COUNTS])
    wait(rows.at[pl.ds(0, (PANELS - 1) * QUARTER), pl.ds(LANES, LANES)], send_sem.at[S_ACROSS])
    wait(slices, send_sem.at[S_CENT])
    to_copy.wait_send()
    wait(least.at[pl.ds(1, PANELS - 1)], send_sem.at[S_LEAST])


def on_device(histograms, first_assign, second_assign, start_centroids):
    vmem = pl.BlockSpec(memory_space=pltpu.VMEM)
    args = [pltpu.with_memory_space_constraint(a, pltpu.HBM) for a in (
        histograms, first_assign.reshape(ROWS // LANES, LANES), second_assign.reshape(ROWS // LANES, LANES),
        start_centroids)]
    cent, dist = pl.pallas_call(
        kernel,
        out_shape=(pltpu.VMEM((PANEL_ROWS, LANES), F32), pltpu.VMEM((1, OUT_ROWS), F32)),
        in_specs=[pl.BlockSpec(memory_space=pltpu.HBM)] * 4,
        out_specs=(vmem, vmem),
        scratch_shapes=[
            pltpu.VMEM((ROWS, 2 * LANES), BF16),
            pltpu.VMEM((ROWS // LANES, LANES), jnp.int32),
            pltpu.VMEM((ROWS // LANES, LANES), jnp.int32),
            pltpu.VMEM((PANEL_ROWS, LANES), F32),
            pltpu.VMEM((OUT_ROWS, 2 * LANES), BF16),
            pltpu.VMEM((2, PANEL_ROWS, 2 * LANES), F32),
            pltpu.VMEM((2, HALF, 2 * LANES), F32),
            pltpu.VMEM((2, CHIPS, OWN, LANES), F32),
            pltpu.VMEM((2, CHIPS - 1, OWN, LANES), F32),
            pltpu.VMEM((2, 1, LANES), F32),
            pltpu.VMEM((CHIPS - 1, 2, 1, LANES), F32),
            pltpu.VMEM((2, PANEL_ROWS, LANES), F32),
            pltpu.VMEM((PANEL_ROWS, 2 * LANES), BF16),
            pltpu.VMEM((PANEL_ROWS, LANES), F32),
            pltpu.VMEM((PANELS, 1, OUT_ROWS), F32),
            pltpu.SemaphoreType.DMA((len(CHUNKS) + 4,)),
            pltpu.SemaphoreType.DMA((N_SEM,)),
            pltpu.SemaphoreType.DMA((N_SEM,)),
            pltpu.SemaphoreType.REGULAR,
            pltpu.SemaphoreType.REGULAR,
        ],
        compiler_params=pltpu.CompilerParams(
            collective_id=0, has_side_effects=True, vmem_limit_bytes=48 * 1024 * 1024),
    )(*args)
    return cent, dist.reshape(OUT_ROWS)


def solution(mesh):
    return jax.shard_map(
        on_device,
        mesh=mesh,
        in_specs=(P("dp", "bin"), P("dp"), P("dp"), P("panel", "bin")),
        out_specs=(P("panel", "bin"), P(("dp", "bin"))),
        check_vma=False,
    )
```

```python
import jax
import jax.numpy as jnp
from jax import lax
from jax.experimental import pallas as pl
from jax.experimental.pallas import tpu as pltpu
from jax.sharding import PartitionSpec as P

MESH = pl.DeviceIdType.MESH
F32, BF16 = jnp.float32, jnp.bfloat16
NYH, NZ, NCORE = 2, 8, 2
CHIPS = NYH * NZ
PANELS = 4
ROWS, LANES = 12288, 128
OUT_ROWS = ROWS // 2
PANEL_ROWS = 256
HALF = PANEL_ROWS // NCORE
OWN = HALF // CHIPS
PRIOR = 384.0
CHUNKS = (2048, 6144, 4096)
TILE = 256
QUARTER = OUT_ROWS // PANELS
PIECES = 8
FIRST = 2
PIECE = QUARTER // PIECES

S_PAIR, S_SUMS, S_ACROSS, S_COUNTS, S_CENT, S_COPY, S_LEAST, S_PIECE = 0, 2, 4, 5, 6, 7, 8, 9
N_SEM = S_PIECE + PIECES


def kernel(hist, first_in, second_in, start_in, cent_out, dist_out,
           hv, first, second, start, rows, acc, sib, red, sums, count, counts, cent, full, norm, least,
           load_sem, send_sem, recv_sem, near_sem, far_sem):
    dp, panel, half_bin = lax.axis_index("dp"), lax.axis_index("panel"), lax.axis_index("bin")
    yh, z, core = dp // (NZ * NCORE), lax.rem(dp // NCORE, NZ), lax.rem(dp, NCORE)
    chip = yh * NZ + z
    other = 1 - core
    bin_peer = 1 - half_bin

    def device(dp_to, panel_to, bin_to):
        return {"dp": dp_to, "panel": panel_to, "bin": bin_to}

    def chip_at(shift):
        yh_to = lax.rem(yh + shift // NZ, NYH)
        return yh_to * NZ + lax.rem(z + shift % NZ, NZ)

    def remote(src, dst, sem, to):
        return pltpu.make_async_remote_copy(
            src_ref=src, dst_ref=dst, send_sem=send_sem.at[sem], recv_sem=recv_sem.at[sem],
            device_id=to, device_id_type=MESH)

    def wait(ref, sem):
        pltpu.make_async_copy(ref, ref, sem).wait()

    sibling = device(chip * NCORE + other, panel, half_bin)
    across = [device(dp, lax.rem(panel + dx, PANELS), half_bin) for dx in (2, 1, 3)]
    shifts = sorted(range(CHIPS), key=lambda s: -min(s % NZ, NZ - s % NZ) - 2 * (s // NZ))
    chips = [chip_at(s) for s in shifts if s]
    same_bin = [device(q * NCORE + core, panel, half_bin) for q in chips]
    other_bin = [device(chip_at(s) * NCORE + core, panel, bin_peer) for s in shifts]

    small = [pltpu.make_async_copy(src, dst, load_sem.at[i])
             for i, (src, dst) in enumerate(((first_in, first), (second_in, second), (start_in, start)))]
    begins = [sum(CHUNKS[:i]) for i in range(len(CHUNKS))]
    loads = [pltpu.make_async_copy(hist.at[pl.ds(at, n)], hv.at[pl.ds(at, n), pl.ds(0, LANES)], load_sem.at[3 + i])
             for i, (at, n) in enumerate(zip(begins, CHUNKS))]
    own_rows = pltpu.make_async_copy(
        hist.at[pl.ds(half_bin * OUT_ROWS, OUT_ROWS)], rows.at[:, pl.ds(0, LANES)], load_sem.at[3 + len(CHUNKS)])
    for copy in small[:2] + loads + small[2:] + [own_rows]:
        copy.start()

    barrier = pltpu.get_barrier_semaphore()
    near = [other_bin[-1]] + across
    far = same_bin + other_bin[:-1]

    def signal(semaphore, to):
        pl.semaphore_signal(semaphore, inc=1, device_id=to, device_id_type=MESH)

    for to in near:
        signal(barrier, device(chip * NCORE, to["panel"], to["bin"]))
    signal(barrier, sibling)
    for to in far:
        signal(barrier, device(to["dp"] - core + 1, to["panel"], to["bin"]))

    def wait_near():
        @pl.when(core == 0)
        def _():
            pl.semaphore_wait(barrier, NCORE * len(near) + 1)
            signal(near_sem, sibling)

        @pl.when(core == 1)
        def _():
            pl.semaphore_wait(near_sem, 1)

    def wait_far():
        @pl.when(core == 1)
        def _():
            pl.semaphore_wait(barrier, NCORE * len(far) + 1)
            signal(far_sem, sibling)

        @pl.when(core == 0)
        def _():
            pl.semaphore_wait(far_sem, 1)

    to_pair = [remote(acc.at[s, pl.ds(pl.multiple_of(other * HALF, HALF), HALF)], sib.at[s], S_PAIR + s, sibling)
               for s in range(2)]

    base = bin_peer * OUT_ROWS
    quarter = panel * QUARTER
    pieces = [remote(hist.at[pl.ds(base + quarter + i * PIECE, PIECE)],
                     rows.at[pl.ds(quarter + i * PIECE, PIECE), pl.ds(LANES, LANES)], S_PIECE + i, other_bin[-1])
              for i in range(PIECES)]

    def pass_on(which):
        for i in which:
            pieces[i].wait_recv()
            at = rows.at[pl.ds(quarter + i * PIECE, PIECE), pl.ds(LANES, LANES)]
            for to in across:
                remote(at, at, S_ACROSS, to).start()

    hv[:, LANES:] = jnp.ones((ROWS, LANES), BF16)

    wait_near()
    for copy in pieces:
        copy.start()

    with jax.named_scope("local_sums"):
        bucket = lax.broadcasted_iota(jnp.int32, (PANEL_ROWS, LANES), 0).astype(F32).astype(BF16)
        one, zero = jnp.ones((), BF16), jnp.zeros((), BF16)
        for copy in small[:2]:
            copy.wait()
        for at, n, load in zip(begins, CHUNKS, loads):
            for s, assign in enumerate((first, second)):
                ids = (assign[at // LANES:(at + n) // LANES, :] - panel * PANEL_ROWS).astype(F32)
                hot = jnp.concatenate([
                    jnp.where(jnp.broadcast_to(ids[j:j + 1, :], (PANEL_ROWS, LANES)).astype(BF16) == bucket, one, zero)
                    for j in range(n // LANES)], axis=1)
                if s == 0:
                    load.wait()
                part = jnp.dot(hot, hv[at:at + n, :], preferred_element_type=F32)
                acc[s] = acc[s] + part if at else part
                if at == begins[-1]:
                    to_pair[s].start()
    pass_on(range(FIRST))
    wait_far()

    with jax.named_scope("chip_sums"):
        own = pl.ds(pl.multiple_of(core * HALF, HALF), HALF)
        diagonal = (lax.broadcasted_iota(jnp.int32, (HALF, LANES), 0)
                    == lax.broadcasted_iota(jnp.int32, (HALF, LANES), 1))
        for s in range(2):
            to_pair[s].wait_recv()
            red[s] = (acc[s, own, :LANES] + sib[s, :, :LANES]).reshape(CHIPS, OWN, LANES)
            count[s] = jnp.sum(jnp.where(diagonal, acc[s, own, LANES:] + sib[s, :, LANES:], 0.0), axis=0, keepdims=True)
            for i, (q, to) in enumerate(zip(chips, same_bin)):
                remote(red.at[s, q], sums.at[s, i], S_SUMS + s, to).start()
                if s:
                    remote(count, counts.at[i], S_COUNTS, to).start()

        pass_on(range(FIRST, PIECES))
        for copy in small[2:]:
            copy.wait()
        wait(counts, recv_sem.at[S_COUNTS])
        number = count[...]
        for i in range(CHIPS - 1):
            number += counts[i]
        mark = (lax.broadcasted_iota(jnp.int32, (OWN, LANES), 1)
                == lax.broadcasted_iota(jnp.int32, (OWN, LANES), 0) + chip * OWN)
        weight = [jnp.sum(jnp.where(mark, jnp.broadcast_to(number[s], (OWN, LANES)), 0.0), axis=1, keepdims=True) + PRIOR
                  for s in range(2)]
        here = pl.ds(pl.multiple_of(core * HALF + chip * OWN, OWN), OWN)
        before = PRIOR * start[here, :]
        wait(sums.at[0], recv_sem.at[S_SUMS])
        total = red[0, chip]
        for i in range(CHIPS - 1):
            total += sums[0, i]
        middle = (total + before) / weight[0]
        wait(sums.at[1], recv_sem.at[S_SUMS + 1])
        total = red[1, chip]
        for i in range(CHIPS - 1):
            total += sums[1, i]
        cent[0, here, :] = (total + PRIOR * middle) / weight[1]

    with jax.named_scope("gather_chips"):
        for i in range(CHIPS):
            remote(cent.at[0, here], cent.at[1, here], S_CENT, other_bin[i]).start()
            if i < CHIPS - 1:
                remote(cent.at[0, here], cent.at[0, here], S_CENT, same_bin[i]).start()
        slices = acc.at[0, pl.ds(0, 2 * HALF - OWN), pl.ds(0, LANES)]
        wait(slices, recv_sem.at[S_CENT])

    with jax.named_scope("gather_cores"):
        mine = pl.ds(pl.multiple_of(core * HALF, HALF), HALF)
        theirs = pl.ds(pl.multiple_of(other * HALF, HALF), HALF)
        to_copy = remote(cent.at[:, mine], cent.at[:, mine], S_COPY, sibling)
        to_copy.start()

        def prepare(at, buckets):
            value = jnp.concatenate([cent[0, at, :], cent[1, at, :]], axis=1)
            full[buckets, :] = (-2.0 * value).astype(BF16)
            norm[buckets, :] = jnp.broadcast_to(jnp.sum(value * value, axis=1, keepdims=True), (HALF, LANES))

        prepare(mine, slice(0, HALF))
        own_rows.wait()
        to_copy.wait_recv()
        prepare(theirs, slice(HALF, PANEL_ROWS))
        wait(rows.at[pl.ds(0, (PANELS - 1) * QUARTER), pl.ds(LANES, LANES)], recv_sem.at[S_ACROSS])

    with jax.named_scope("least"):
        for t in range(OUT_ROWS // TILE):
            dots = lax.dot_general(full[...], rows[t * TILE:(t + 1) * TILE, :], (((1,), (1,)), ((), ())),
                                   preferred_element_type=F32)
            value = dots + jnp.concatenate([norm[...]] * (TILE // LANES), axis=1)
            least[0, :, t * TILE:(t + 1) * TILE] = jnp.min(value, axis=0, keepdims=True)
            if (t + 1) * TILE in (OUT_ROWS // 2, OUT_ROWS):
                part = pl.ds((t + 1) * TILE - OUT_ROWS // 2, OUT_ROWS // 2)
                for dx, to in zip((2, 1, 3), across):
                    remote(least.at[0, :, part], least.at[dx, :, part], S_LEAST, to).start()
        cent_out[...] = cent[0]
        wait(least.at[pl.ds(1, PANELS - 1)], recv_sem.at[S_LEAST])
        dist_out[...] = jnp.minimum(jnp.minimum(least[0], least[1]), jnp.minimum(least[2], least[3]))

    for copy in to_pair:
        copy.wait_send()
    for copy in pieces:
        copy.wait_send()
    for s in range(2):
        wait(sums.at[s], send_sem.at[S_SUMS + s])
    wait(counts, send_sem.at[S_COUNTS])
    wait(rows.at[pl.ds(0, (PANELS - 1) * QUARTER), pl.ds(LANES, LANES)], send_sem.at[S_ACROSS])
    wait(slices, send_sem.at[S_CENT])
    to_copy.wait_send()
    wait(least.at[pl.ds(1, PANELS - 1)], send_sem.at[S_LEAST])


def on_device(histograms, first_assign, second_assign, start_centroids):
    vmem = pl.BlockSpec(memory_space=pltpu.VMEM)
    args = [pltpu.with_memory_space_constraint(a, pltpu.HBM) for a in (
        histograms, first_assign.reshape(ROWS // LANES, LANES), second_assign.reshape(ROWS // LANES, LANES),
        start_centroids)]
    cent, dist = pl.pallas_call(
        kernel,
        out_shape=(pltpu.VMEM((PANEL_ROWS, LANES), F32), pltpu.VMEM((1, OUT_ROWS), F32)),
        in_specs=[pl.BlockSpec(memory_space=pltpu.HBM)] * 4,
        out_specs=(vmem, vmem),
        scratch_shapes=[
            pltpu.VMEM((ROWS, 2 * LANES), BF16),
            pltpu.VMEM((ROWS // LANES, LANES), jnp.int32),
            pltpu.VMEM((ROWS // LANES, LANES), jnp.int32),
            pltpu.VMEM((PANEL_ROWS, LANES), F32),
            pltpu.VMEM((OUT_ROWS, 2 * LANES), BF16),
            pltpu.VMEM((2, PANEL_ROWS, 2 * LANES), F32),
            pltpu.VMEM((2, HALF, 2 * LANES), F32),
            pltpu.VMEM((2, CHIPS, OWN, LANES), F32),
            pltpu.VMEM((2, CHIPS - 1, OWN, LANES), F32),
            pltpu.VMEM((2, 1, LANES), F32),
            pltpu.VMEM((CHIPS - 1, 2, 1, LANES), F32),
            pltpu.VMEM((2, PANEL_ROWS, LANES), F32),
            pltpu.VMEM((PANEL_ROWS, 2 * LANES), BF16),
            pltpu.VMEM((PANEL_ROWS, LANES), F32),
            pltpu.VMEM((PANELS, 1, OUT_ROWS), F32),
            pltpu.SemaphoreType.DMA((len(CHUNKS) + 4,)),
            pltpu.SemaphoreType.DMA((N_SEM,)),
            pltpu.SemaphoreType.DMA((N_SEM,)),
            pltpu.SemaphoreType.REGULAR,
            pltpu.SemaphoreType.REGULAR,
        ],
        compiler_params=pltpu.CompilerParams(
            collective_id=0, has_side_effects=True, vmem_limit_bytes=48 * 1024 * 1024),
    )(*args)
    return cent, dist.reshape(OUT_ROWS)


def solution(mesh):
    return jax.shard_map(
        on_device,
        mesh=mesh,
        in_specs=(P("dp", "bin"), P("dp"), P("dp"), P("panel", "bin")),
        out_specs=(P("panel", "bin"), P(("dp", "bin"))),
        check_vma=False,
    )
```

```python
import jax
import jax.numpy as jnp
from jax import lax
from jax.experimental import pallas as pl
from jax.experimental.pallas import tpu as pltpu
from jax.sharding import PartitionSpec as P

MESH = pl.DeviceIdType.MESH
F32, BF16 = jnp.float32, jnp.bfloat16
NYH, NZ, NCORE = 2, 8, 2
CHIPS = NYH * NZ
PANELS = 4
ROWS, LANES = 12288, 128
OUT_ROWS = ROWS // 2
PANEL_ROWS = 256
HALF = PANEL_ROWS // NCORE
OWN = HALF // CHIPS
PRIOR = 384.0
CHUNKS = (2048, 6144, 4096)
TILE = 256
QUARTER = OUT_ROWS // PANELS
PIECES = 8
FIRST = 2
PIECE = QUARTER // PIECES

S_PAIR, S_SUMS, S_CENT, S_COPY, S_ACROSS, S_COUNTS, S_LEAST, S_PIECE = 0, 2, 4, 6, 8, 9, 10, 11
N_SEM = S_PIECE + PIECES


def kernel(hist, first_in, second_in, start_in, cent_out, dist_out,
           hv, first, second, start, rows, acc, sib, red, sums, count, counts, cent, full, norm, least,
           load_sem, send_sem, recv_sem, near_sem, far_sem):
    dp, panel, half_bin = lax.axis_index("dp"), lax.axis_index("panel"), lax.axis_index("bin")
    yh, z, core = dp // (NZ * NCORE), lax.rem(dp // NCORE, NZ), lax.rem(dp, NCORE)
    chip = yh * NZ + z
    other = 1 - core
    bin_peer = 1 - half_bin

    def device(dp_to, panel_to, bin_to):
        return {"dp": dp_to, "panel": panel_to, "bin": bin_to}

    def chip_at(shift):
        yh_to = lax.rem(yh + shift // NZ, NYH)
        return yh_to * NZ + lax.rem(z + shift % NZ, NZ)

    def remote(src, dst, sem, to):
        return pltpu.make_async_remote_copy(
            src_ref=src, dst_ref=dst, send_sem=send_sem.at[sem], recv_sem=recv_sem.at[sem],
            device_id=to, device_id_type=MESH)

    def wait(ref, sem):
        pltpu.make_async_copy(ref, ref, sem).wait()

    sibling = device(chip * NCORE + other, panel, half_bin)
    across = [device(dp, lax.rem(panel + dx, PANELS), half_bin) for dx in (2, 1, 3)]
    shifts = sorted(range(CHIPS), key=lambda s: -min(s % NZ, NZ - s % NZ) - 2 * (s // NZ))
    chips = [chip_at(s) for s in shifts if s]
    same_bin = [device(q * NCORE + core, panel, half_bin) for q in chips]
    other_bin = [device(chip_at(s) * NCORE + core, panel, bin_peer) for s in shifts]

    small = [pltpu.make_async_copy(src, dst, load_sem.at[i])
             for i, (src, dst) in enumerate(((first_in, first), (second_in, second), (start_in, start)))]
    begins = [sum(CHUNKS[:i]) for i in range(len(CHUNKS))]
    loads = [pltpu.make_async_copy(hist.at[pl.ds(at, n)], hv.at[pl.ds(at, n), pl.ds(0, LANES)], load_sem.at[3 + i])
             for i, (at, n) in enumerate(zip(begins, CHUNKS))]
    own_rows = pltpu.make_async_copy(
        hist.at[pl.ds(half_bin * OUT_ROWS, OUT_ROWS)], rows.at[:, pl.ds(0, LANES)], load_sem.at[3 + len(CHUNKS)])
    for copy in small[:2] + loads + small[2:] + [own_rows]:
        copy.start()

    barrier = pltpu.get_barrier_semaphore()
    near = [other_bin[-1]] + across
    far = same_bin + other_bin[:-1]

    def signal(semaphore, to):
        pl.semaphore_signal(semaphore, inc=1, device_id=to, device_id_type=MESH)

    for to in near:
        signal(barrier, device(chip * NCORE, to["panel"], to["bin"]))
    signal(barrier, sibling)
    for to in far:
        signal(barrier, device(to["dp"] - core + 1, to["panel"], to["bin"]))

    def wait_near():
        @pl.when(core == 0)
        def _():
            pl.semaphore_wait(barrier, NCORE * len(near) + 1)
            signal(near_sem, sibling)

        @pl.when(core == 1)
        def _():
            pl.semaphore_wait(near_sem, 1)

    def wait_far():
        @pl.when(core == 1)
        def _():
            pl.semaphore_wait(barrier, NCORE * len(far) + 1)
            signal(far_sem, sibling)

        @pl.when(core == 0)
        def _():
            pl.semaphore_wait(far_sem, 1)

    to_pair = [remote(acc.at[s, pl.ds(pl.multiple_of(other * HALF, HALF), HALF)], sib.at[s], S_PAIR + s, sibling)
               for s in range(2)]

    base = bin_peer * OUT_ROWS
    quarter = panel * QUARTER
    pieces = [remote(hist.at[pl.ds(base + quarter + i * PIECE, PIECE)],
                     rows.at[pl.ds(quarter + i * PIECE, PIECE), pl.ds(LANES, LANES)], S_PIECE + i, other_bin[-1])
              for i in range(PIECES)]

    def pass_on(which):
        for i in which:
            pieces[i].wait_recv()
            at = rows.at[pl.ds(quarter + i * PIECE, PIECE), pl.ds(LANES, LANES)]
            for to in across:
                remote(at, at, S_ACROSS, to).start()

    hv[:, LANES:] = jnp.ones((ROWS, LANES), BF16)

    wait_near()
    for copy in pieces:
        copy.start()

    with jax.named_scope("local_sums"):
        bucket = lax.broadcasted_iota(jnp.int32, (PANEL_ROWS, LANES), 0).astype(F32).astype(BF16)
        one, zero = jnp.ones((), BF16), jnp.zeros((), BF16)
        for copy in small[:2]:
            copy.wait()
        for at, n, load in zip(begins, CHUNKS, loads):
            for s, assign in enumerate((first, second)):
                ids = (assign[at // LANES:(at + n) // LANES, :] - panel * PANEL_ROWS).astype(F32)
                hot = jnp.concatenate([
                    jnp.where(jnp.broadcast_to(ids[j:j + 1, :], (PANEL_ROWS, LANES)).astype(BF16) == bucket, one, zero)
                    for j in range(n // LANES)], axis=1)
                if s == 0:
                    load.wait()
                part = jnp.dot(hot, hv[at:at + n, :], preferred_element_type=F32)
                acc[s] = acc[s] + part if at else part
                if at == begins[-1]:
                    to_pair[s].start()
    pass_on(range(FIRST))
    wait_far()

    with jax.named_scope("chip_sums"):
        own = pl.ds(pl.multiple_of(core * HALF, HALF), HALF)
        diagonal = (lax.broadcasted_iota(jnp.int32, (HALF, LANES), 0)
                    == lax.broadcasted_iota(jnp.int32, (HALF, LANES), 1))
        for s in range(2):
            to_pair[s].wait_recv()
            red[s] = (acc[s, own, :LANES] + sib[s, :, :LANES]).reshape(CHIPS, OWN, LANES)
            count[s] = jnp.sum(jnp.where(diagonal, acc[s, own, LANES:] + sib[s, :, LANES:], 0.0), axis=0, keepdims=True)
            for i, (q, to) in enumerate(zip(chips, same_bin)):
                remote(red.at[s, q], sums.at[s, i], S_SUMS + s, to).start()
                if s:
                    remote(count, counts.at[i], S_COUNTS, to).start()

        pass_on(range(FIRST, PIECES))
        for copy in small[2:]:
            copy.wait()
        wait(counts, recv_sem.at[S_COUNTS])
        number = count[...]
        for i in range(CHIPS - 1):
            number += counts[i]
        mark = (lax.broadcasted_iota(jnp.int32, (OWN, LANES), 1)
                == lax.broadcasted_iota(jnp.int32, (OWN, LANES), 0) + chip * OWN)
        weight = [jnp.sum(jnp.where(mark, jnp.broadcast_to(number[s], (OWN, LANES)), 0.0), axis=1, keepdims=True) + PRIOR
                  for s in range(2)]
        here = pl.ds(pl.multiple_of(core * HALF + chip * OWN, OWN), OWN)
        before = PRIOR * start[here, :]
        wait(sums.at[0], recv_sem.at[S_SUMS])
        total = red[0, chip]
        for i in range(CHIPS - 1):
            total += sums[0, i]
        middle = (total + before) / weight[0]
        wait(sums.at[1], recv_sem.at[S_SUMS + 1])
        total = red[1, chip]
        for i in range(CHIPS - 1):
            total += sums[1, i]
        cent[0, here, :] = (total + PRIOR * middle) / weight[1]

    with jax.named_scope("gather_chips"):
        for to in same_bin:
            remote(cent.at[0, here], cent.at[0, here], S_CENT, to).start()
        for to in other_bin:
            remote(cent.at[0, here], cent.at[1, here], S_CENT + 1, to).start()
        slices = [acc.at[0, pl.ds(0, HALF - OWN), pl.ds(0, LANES)], acc.at[0, pl.ds(0, HALF), pl.ds(0, LANES)]]

    with jax.named_scope("gather_cores"):
        mine = pl.ds(pl.multiple_of(core * HALF, HALF), HALF)
        theirs = pl.ds(pl.multiple_of(other * HALF, HALF), HALF)
        to_copy = [remote(cent.at[b, mine], cent.at[b, mine], S_COPY + b, sibling) for b in range(2)]
        for b in range(2):
            wait(slices[b], recv_sem.at[S_CENT + b])
            to_copy[b].start()

        def prepare(at, buckets):
            value = jnp.concatenate([cent[0, at, :], cent[1, at, :]], axis=1)
            full[buckets, :] = (-2.0 * value).astype(BF16)
            norm[buckets, :] = jnp.broadcast_to(jnp.sum(value * value, axis=1, keepdims=True), (HALF, LANES))

        prepare(mine, slice(0, HALF))
        own_rows.wait()
        for copy in to_copy:
            copy.wait_recv()
        prepare(theirs, slice(HALF, PANEL_ROWS))
        wait(rows.at[pl.ds(0, (PANELS - 1) * QUARTER), pl.ds(LANES, LANES)], recv_sem.at[S_ACROSS])

    with jax.named_scope("least"):
        for t in range(OUT_ROWS // TILE):
            dots = lax.dot_general(full[...], rows[t * TILE:(t + 1) * TILE, :], (((1,), (1,)), ((), ())),
                                   preferred_element_type=F32)
            value = dots + jnp.concatenate([norm[...]] * (TILE // LANES), axis=1)
            least[0, :, t * TILE:(t + 1) * TILE] = jnp.min(value, axis=0, keepdims=True)
            if (t + 1) * TILE in (OUT_ROWS // 2, OUT_ROWS):
                part = pl.ds((t + 1) * TILE - OUT_ROWS // 2, OUT_ROWS // 2)
                for dx, to in zip((2, 1, 3), across):
                    remote(least.at[0, :, part], least.at[dx, :, part], S_LEAST, to).start()
        cent_out[...] = cent[0]
        wait(least.at[pl.ds(1, PANELS - 1)], recv_sem.at[S_LEAST])
        dist_out[...] = jnp.minimum(jnp.minimum(least[0], least[1]), jnp.minimum(least[2], least[3]))

    for copy in to_pair:
        copy.wait_send()
    for copy in pieces:
        copy.wait_send()
    for s in range(2):
        wait(sums.at[s], send_sem.at[S_SUMS + s])
    wait(counts, send_sem.at[S_COUNTS])
    wait(rows.at[pl.ds(0, (PANELS - 1) * QUARTER), pl.ds(LANES, LANES)], send_sem.at[S_ACROSS])
    for b in range(2):
        wait(slices[b], send_sem.at[S_CENT + b])
        to_copy[b].wait_send()
    wait(least.at[pl.ds(1, PANELS - 1)], send_sem.at[S_LEAST])


def on_device(histograms, first_assign, second_assign, start_centroids):
    vmem = pl.BlockSpec(memory_space=pltpu.VMEM)
    args = [pltpu.with_memory_space_constraint(a, pltpu.HBM) for a in (
        histograms, first_assign.reshape(ROWS // LANES, LANES), second_assign.reshape(ROWS // LANES, LANES),
        start_centroids)]
    cent, dist = pl.pallas_call(
        kernel,
        out_shape=(pltpu.VMEM((PANEL_ROWS, LANES), F32), pltpu.VMEM((1, OUT_ROWS), F32)),
        in_specs=[pl.BlockSpec(memory_space=pltpu.HBM)] * 4,
        out_specs=(vmem, vmem),
        scratch_shapes=[
            pltpu.VMEM((ROWS, 2 * LANES), BF16),
            pltpu.VMEM((ROWS // LANES, LANES), jnp.int32),
            pltpu.VMEM((ROWS // LANES, LANES), jnp.int32),
            pltpu.VMEM((PANEL_ROWS, LANES), F32),
            pltpu.VMEM((OUT_ROWS, 2 * LANES), BF16),
            pltpu.VMEM((2, PANEL_ROWS, 2 * LANES), F32),
            pltpu.VMEM((2, HALF, 2 * LANES), F32),
            pltpu.VMEM((2, CHIPS, OWN, LANES), F32),
            pltpu.VMEM((2, CHIPS - 1, OWN, LANES), F32),
            pltpu.VMEM((2, 1, LANES), F32),
            pltpu.VMEM((CHIPS - 1, 2, 1, LANES), F32),
            pltpu.VMEM((2, PANEL_ROWS, LANES), F32),
            pltpu.VMEM((PANEL_ROWS, 2 * LANES), BF16),
            pltpu.VMEM((PANEL_ROWS, LANES), F32),
            pltpu.VMEM((PANELS, 1, OUT_ROWS), F32),
            pltpu.SemaphoreType.DMA((len(CHUNKS) + 4,)),
            pltpu.SemaphoreType.DMA((N_SEM,)),
            pltpu.SemaphoreType.DMA((N_SEM,)),
            pltpu.SemaphoreType.REGULAR,
            pltpu.SemaphoreType.REGULAR,
        ],
        compiler_params=pltpu.CompilerParams(
            collective_id=0, has_side_effects=True, vmem_limit_bytes=48 * 1024 * 1024),
    )(*args)
    return cent, dist.reshape(OUT_ROWS)


def solution(mesh):
    return jax.shard_map(
        on_device,
        mesh=mesh,
        in_specs=(P("dp", "bin"), P("dp"), P("dp"), P("panel", "bin")),
        out_specs=(P("panel", "bin"), P(("dp", "bin"))),
        check_vma=False,
    )
```
